32 devices in a mesh: slab: 2 (over x), tile: 8 (over z, y), ch: 2 (over core).
Axes of the slice: x: 2, y: 2, z: 4, core: 2. Of those that a mesh axis runs over, the one named last changes fastest.
Arguments:
- volume: bfloat16 [4, 128, 1024], P('slab', 'tile'), may hold values from -6 to 6
- xz_tissue: int32 [128], P('tile'), may hold values 0 or 1
- yz_tissue: int32 [1024], P(('slab', 'tile')), may hold values 0 or 1
- first_conv: bfloat16 [32, 9, 1], replicated, may hold values from -2 to 2
- second_conv: bfloat16 [32, 9, 32], replicated, may hold values from -0.375 to 0.375
- third_conv: bfloat16 [64, 9, 32], replicated, may hold values from -0.375 to 0.375
- fourth_conv: bfloat16 [64, 9, 64], replicated, may hold values from -0.25 to 0.25
- fifth_conv: bfloat16 [32, 9, 96], replicated, may hold values from -0.21875 to 0.21875
- sixth_conv: bfloat16 [32, 9, 32], replicated, may hold values from -0.375 to 0.375
- out_weight: bfloat16 [32], replicated, may hold values from -1 to 1
Outputs:
- restored: bfloat16 [4, 128, 1024], P('slab', 'tile')
The draws below stay inside these ranges and needn't reach their ends.
All inputs are finite; a program needn't handle non-finite values. No bound on the sum of `xz_tissue` or of `yz_tissue` on one device may be relied on, other than what follows from the above.
Results may differ from the reference program's by a relative error of at most 0.0037.
Values may be sent and summed in bfloat16 or wider, within the bound.
A program may use at most 128 MiB of HBM per device.

```python
import jax
import jax.numpy as jnp
from jax import lax

C1 = 32
C2 = 64
X = 1024
Z = 4
Y = 128


def plant(array, own_key, smallest, high):
    longest = array.shape.index(max(array.shape))
    spots = []
    for shift in (0, 1):
        where = [jax.random.randint(jax.random.fold_in(own_key, axis), (), 0, length) for axis, length in enumerate(array.shape)]
        where[longest] = (where[longest] + shift) % array.shape[longest]
        spots.append(tuple(where))
    return array.at[spots[0]].set(smallest).at[spots[1]].set(high)


def levels(own_key, extent, shards, smallest, top_value):
    factor_of = 1.0
    for dim, blocks in shards:
        draws = jax.random.uniform(jax.random.fold_in(jax.random.fold_in(own_key, 6), dim), (blocks,), jnp.float32, smallest / len(shards), top_value / len(shards))
        factor_of = factor_of * jnp.repeat(jnp.exp(draws), extent[dim] // blocks).reshape((-1,) + (1,) * (len(extent) - 1 - dim))
    return factor_of


def gaussian(stream_key, extent, width, most, split=(), held_as=jnp.bfloat16):
    loudness = levels(stream_key, extent, split, -0.22, 0.18) if split else 1.0
    drawn = jax.random.normal(stream_key, extent, jnp.float32) * width * loudness
    return jnp.minimum(jnp.maximum(drawn, -most), most).astype(held_as)


def setup_inputs(seed: int = 0) -> dict:
    splits = jax.random.split(jax.random.key(seed), 11)
    volume = gaussian(splits[0], (Z, Y, X), 1.0, 6.0, ((0, 2), (1, 8)))
    xz_tissue = plant((jax.random.randint(splits[1], (Y,), 0, 2) < 1).astype(jnp.int32), jax.random.fold_in(splits[1], 1), 0, 1)
    yz_tissue = plant((jax.random.randint(splits[2], (X,), 0, 2) < 1).astype(jnp.int32), jax.random.fold_in(splits[2], 1), 0, 1)
    first_conv = gaussian(splits[3], (C1, 9, 1), 9 ** -0.5, 2.0)
    second_conv = gaussian(splits[4], (C1, 9, C1), (9 * C1) ** -0.5, 0.375)
    third_conv = gaussian(splits[5], (C2, 9, C1), (9 * C1) ** -0.5, 0.375)
    fourth_conv = gaussian(splits[6], (C2, 9, C2), (9 * C2) ** -0.5, 0.25)
    fifth_conv = gaussian(splits[7], (C1, 9, C2 + C1), (9 * (C2 + C1)) ** -0.5, 0.21875)
    sixth_conv = gaussian(splits[8], (C1, 9, C1), (9 * C1) ** -0.5, 0.375)
    out_weight = gaussian(splits[9], (C1,), C1 ** -0.5, 1.0)
    return {"volume": volume, "xz_tissue": xz_tissue, "yz_tissue": yz_tissue, "first_conv": first_conv, "second_conv": second_conv, "third_conv": third_conv, "fourth_conv": fourth_conv, "fifth_conv": fifth_conv, "sixth_conv": sixth_conv, "out_weight": out_weight}


def convolve(signal, weight):
    channels, height, breadth = signal.shape
    padded = jnp.pad(signal, ((0, 0), (1, 1), (1, 1)))
    stacked = jnp.stack([padded[:, row_shift:row_shift + height, col_shift:col_shift + breadth] for row_shift in range(3) for col_shift in range(3)], axis=0)
    stacked = stacked.reshape(9 * channels, height, breadth).astype(jnp.float32)
    matrix = weight.reshape(weight.shape[0], 9 * channels).astype(jnp.float32)
    return jnp.einsum("ok,khw->ohw", matrix, stacked)


def activate(signal, weight):
    return jax.nn.relu(convolve(signal, weight)).astype(jnp.bfloat16)


def shrink(signal):
    channels, height, breadth = signal.shape
    blocks = signal.astype(jnp.float32).reshape(channels, height // 2, 2, breadth // 2, 2)
    return jnp.mean(blocks, axis=(2, 4)).astype(jnp.bfloat16)


def enlarge(signal):
    return jnp.repeat(jnp.repeat(signal, 2, axis=1), 2, axis=2)


def network(picture, weights):
    first_conv, second_conv, third_conv, fourth_conv, fifth_conv, sixth_conv, out_weight = weights
    opening = activate(picture[None], first_conv)
    skipped = activate(opening, second_conv)
    coarse = activate(shrink(skipped), third_conv)
    coarse = activate(coarse, fourth_conv)
    joined = jnp.concatenate([enlarge(coarse), skipped], axis=0)
    refined = activate(joined, fifth_conv)
    refined = activate(refined, sixth_conv)
    head = jnp.einsum("c,chw->hw", out_weight.astype(jnp.float32), refined.astype(jnp.float32))
    return picture.astype(jnp.float32) + head


def restore(planes, tissue, weights):
    def single(entry):
        picture, marker = entry
        value_new = network(picture, weights)
        return jnp.where(marker > 0, value_new, picture.astype(jnp.float32)).astype(jnp.bfloat16)

    return lax.map(single, (planes, tissue))


def reference(volume, xz_tissue, yz_tissue, first_conv, second_conv, third_conv, fourth_conv, fifth_conv, sixth_conv, out_weight):
    weights = (first_conv, second_conv, third_conv, fourth_conv, fifth_conv, sixth_conv, out_weight)
    xz_result = restore(jnp.transpose(volume, (1, 0, 2)), xz_tissue, weights)
    xz_result = jnp.transpose(xz_result, (1, 0, 2))
    yz_result = restore(jnp.transpose(volume, (2, 0, 1)), yz_tissue, weights)
    yz_result = jnp.transpose(yz_result, (1, 2, 0))
    averaged = 0.5 * (xz_result.astype(jnp.float32) + yz_result.astype(jnp.float32))
    return averaged.astype(jnp.bfloat16)
```

```python
import functools

import jax
import jax.numpy as jnp
from jax import lax
from jax.experimental import pallas as pl
from jax.experimental.pallas import tpu as pltpu
from jax.sharding import PartitionSpec as P

MESH = pl.DeviceIdType.MESH
HALO = 8
GROUP = 64
BLOCK = 16
BF = jnp.bfloat16
F32 = jnp.float32


def iota(shape, axis):
    return lax.broadcasted_iota(jnp.int32, shape, axis)


def dot(a, b):
    return jnp.dot(a, b, preferred_element_type=F32)


def spread(wide, taps):
    count, outs = taps.shape
    lanes = wide.shape[1]
    repeat = jnp.where(iota((outs, lanes), 1) % outs == iota((outs, lanes), 0), 1.0, 0.0)
    wide[0:count, :] = dot(taps, repeat.astype(BF))


def band(dst, row, wide, depth, first, count, lanes, half, outs, pick):
    lane = iota((1, lanes), 1)
    p, zo = lane // half, (lane % half) // outs
    total = jnp.zeros((count, lanes), F32)
    for r in range(3):
        for s in range(3):
            hit = pick(p, zo, r, s)
            if hit is None:
                continue
            start = (3 * r + s) * depth + first
            total = total + jnp.where(hit, wide[start : start + count, :], 0.0)
    dst[row : row + count, :] = total.astype(BF)


def plain_pick(q, zi):
    def pick(p, zo, r, s):
        if s not in (q, q - 1):
            return None
        return (p == q - s) & (zo == zi + 1 - r)

    return pick


def up_pick(d, zp, levels):
    def pick(p, zo, r, s):
        z = zo + r - 1
        return ((p + s + 1) // 2 - 1 == d) & (z >= 0) & (z < levels) & (z // 2 == zp)

    return pick


def kernel(
    slabs, tiles, chs,
    vol, xz_flag, yz_flag, k1, k2, k3, k4, k5, k6, tail,
    out,
    vxz, ryz, turned, w1, w2, w3, w4, w5, w6,
    e1, e2, pooled, m1, m2, wide,
    xr, yt, place, rx, ry,
    in_local, xin_send, xin_recv, yin_send, yin_recv,
    xo_send, xo_recv, yo_send, yo_recv,
):
    d1, d2 = e1, e2
    zd, yd, across = vol.shape
    levels = slabs * zd
    breadth = tiles * yd
    devices = slabs * tiles * chs
    half = 32 * levels
    full = 2 * half
    small = half <= 128
    window = 4 * levels
    per_chunk = 128 // window
    width = across // (slabs * chs)
    cols = across // devices
    rows_y = max(16, cols)
    s, t, c = lax.axis_index("slab"), lax.axis_index("tile"), lax.axis_index("ch")
    g = s * chs + c
    me = (s * tiles + t) * chs + c

    def coords(k):
        return k // (tiles * chs), (k // chs) % tiles, k % chs

    def others(body):
        def step(k, carry):
            @pl.when(k != me)
            def _():
                body(k)

            return carry

        lax.fori_loop(0, devices, step, 0)

    barrier = pltpu.get_barrier_semaphore()

    def greet(k):
        ks, kt, kc = coords(k)
        pl.semaphore_signal(
            barrier, inc=1, device_id={"slab": ks, "tile": kt, "ch": kc}, device_id_type=MESH
        )

    others(greet)
    pl.semaphore_wait(barrier, devices - 1)

    def xin(k):
        return pltpu.make_async_remote_copy(
            src_ref=vol,
            dst_ref=vxz.at[pl.ds(s * zd, zd), :, pl.ds(128, across)],
            send_sem=xin_send.at[k],
            recv_sem=xin_recv.at[s],
            device_id={"slab": k, "tile": t, "ch": c},
            device_id_type=MESH,
        )

    def xin_from(k):
        return pltpu.make_async_remote_copy(
            src_ref=vol,
            dst_ref=vxz.at[pl.ds(k * zd, zd), :, pl.ds(128, across)],
            send_sem=xin_send.at[k],
            recv_sem=xin_recv.at[k],
            device_id={"slab": k, "tile": t, "ch": c},
            device_id_type=MESH,
        )

    def lanes_of(k):
        return pl.ds(pl.multiple_of((k * cols * chs) // 128 * 128, 128), 128)

    def yin(k):
        ks, kt = k // tiles, k % tiles
        return pltpu.make_async_remote_copy(
            src_ref=vol.at[:, :, lanes_of(k)],
            dst_ref=ryz.at[t, s],
            send_sem=yin_send.at[k],
            recv_sem=yin_recv.at[s * tiles + t],
            device_id={"slab": ks, "tile": kt, "ch": c},
            device_id_type=MESH,
        )

    def yin_from(k):
        ks, kt = k // tiles, k % tiles
        return pltpu.make_async_remote_copy(
            src_ref=vol.at[:, :, lanes_of(k)],
            dst_ref=ryz.at[kt, ks],
            send_sem=yin_send.at[k],
            recv_sem=yin_recv.at[k],
            device_id={"slab": ks, "tile": kt, "ch": c},
            device_id_type=MESH,
        )

    def loop(count, own, body):
        def step(k, carry):
            @pl.when(k != own)
            def _():
                body(k)

            return carry

        lax.fori_loop(0, count, step, 0)

    place_me = s * tiles + t
    loop(slabs, s, lambda k: xin(k).start())
    loop(slabs * tiles, place_me, lambda k: yin(k).start())
    own_x = pltpu.make_async_copy(
        vol, vxz.at[pl.ds(s * zd, zd), :, pl.ds(128, across)], in_local.at[0]
    )
    own_y = pltpu.make_async_copy(vol.at[:, :, lanes_of(place_me)], ryz.at[t, s], in_local.at[1])
    own_x.start()
    own_y.start()

    edge = jnp.zeros((levels, yd, 128), BF)
    vxz[:, :, 0:128] = edge
    vxz[:, :, 128 + across :] = edge

    spread(wide, k1[...])
    line, lane = iota((window, full), 0), iota((window, full), 1)
    base = jnp.zeros((window, full), F32)
    for r in range(3):
        for q in range(3):
            hit = (line // levels - lane // half == q) & (
                line % levels - (lane % half) // 32 + 1 == r
            )
            base = base + jnp.where(hit, wide[3 * r + q : 3 * r + q + 1, :], 0.0)
    base = base.astype(BF)
    w1[...] = jnp.zeros(w1.shape, BF)
    for m in range(per_chunk):
        w1[m * window : (m + 1) * window, m * full : (m + 1) * full] = base

    order = (1, 2, 0, 3)
    for kk, ww in ((k2, w2), (k6, w6)):
        spread(wide, kk[...])
        for n, q in enumerate(order):
            for zi in range(levels):
                band(ww, n * half + 32 * zi, wide, 32, 0, 32, full, half, 32, plain_pick(q, zi))
    spread(wide, k3[...])
    for n, q in enumerate(order):
        for zi in range(levels // 2):
            band(w3, n * half + 64 * zi, wide, 32, 0, 32, full, half, 64, plain_pick(q, zi))
            w3[n * half + 64 * zi + 32 : n * half + 64 * zi + 64, :] = jnp.zeros((32, full), BF)
    spread(wide, k4[...])
    for n, q in enumerate(order):
        for zi in range(levels // 2):
            band(w4, n * half + 64 * zi, wide, 64, 0, 64, full, half, 64, plain_pick(q, zi))
    spread(wide, k5[...])
    for n, q in enumerate(order):
        for zi in range(levels):
            band(w5, n * half + 32 * zi, wide, 96, 64, 32, full, half, 32, plain_pick(q, zi))
    for n, d in enumerate((-1, 0, 1)):
        for zp in range(levels // 2):
            band(
                w5, (4 + n) * half + 64 * zp, wide, 96, 0, 64, full, half, 32,
                up_pick(d, zp, levels),
            )

    def pieces(count, rows):
        best = 1
        for n in range(1, count + 1):
            if count % n == 0 and count // n * rows * half >= 384 * 128:
                best = n
        return best

    def ranged(lo, hi, rows, body):
        n = pieces(hi - lo, rows)
        size = (hi - lo) // n
        for i in range(n):
            body(lo + i * size, size)

    def around(src, a, n):
        return [
            src[a + 1 : a + 1 + n],
            src[a : a + n][:, :, half:],
            src[a + 2 : a + 2 + n][:, :, :half],
        ]

    def conv(parts, weight, n, rows):
        joined = jnp.concatenate(parts, axis=-1)
        joined = joined.reshape(n * rows, joined.shape[-1])
        return jnp.maximum(dot(joined, weight[...]), 0.0).astype(BF).reshape(n, rows, full)

    def network(u, rows, pairs, margin, clear):
        chunks = pairs // per_chunk
        for ref in (e1, e2):
            z1 = jnp.zeros((1, rows, full), BF)
            ref[0:1, 0:rows] = z1
            ref[pairs + 1 : pairs + 2, 0:rows] = z1
        for ref in (pooled, m1):
            z1 = jnp.zeros((1, rows, full), BF)
            ref[0:1, 0:rows] = z1
            ref[pairs // 2 + 1 : pairs // 2 + 2, 0:rows] = z1
        z1 = jnp.zeros((1, rows, half), BF)
        m2[0:1, 0:rows] = z1
        m2[pairs + 1 : pairs + 2, 0:rows] = z1
        flat = u.reshape(chunks * rows, 128)
        for m in range(per_chunk):
            got = jnp.maximum(dot(flat, w1[:, m * full : (m + 1) * full]), 0.0).astype(BF)
            got = got.reshape(chunks, rows, full)
            for i in range(chunks):
                e1[i * per_chunk + m + 1, 0:rows] = got[i]
        clear(e1)
        need = margin // 2

        def second(a, n):
            parts = [x[:, 0:rows] for x in around(e1, a, n)]
            got = conv(parts, w2, n, rows)
            e2[a + 1 : a + 1 + n, 0:rows] = got

        ranged(need, pairs - need, rows, second)
        clear(e2)

        def shrink(a, n):
            x = e2[2 * a + 1 : 2 * a + 1 + 2 * n, 0:rows].astype(F32)
            x = (x[:, :, :half] + x[:, :, half:]).reshape(2 * n * rows, half)
            x = (x + pltpu.roll(x, half - 32, axis=1)) * 0.25
            x = x.astype(BF).reshape(n, 2, rows, half)
            pooled[a + 1 : a + 1 + n, 0:rows] = jnp.concatenate([x[:, 0], x[:, 1]], axis=-1)

        ranged(need // 2, pairs // 2 - need // 2, rows, shrink)

        def third(a, n):
            parts = [x[:, 0:rows] for x in around(pooled, a, n)]
            m1[a + 1 : a + 1 + n, 0:rows] = conv(parts, w3, n, rows)

        ranged(need // 2, pairs // 2 - need // 2, rows, third)
        clear(m1, 2)

        def fourth(a, n):
            parts = [x[:, 0:rows] for x in around(m1, a, n)]
            got = conv(parts, w4, n, rows)
            for i in range(n):
                m2[2 * (a + i) + 1, 0:rows] = got[i, :, :half]
                m2[2 * (a + i) + 2, 0:rows] = got[i, :, half:]

        ranged(need // 2, pairs // 2 - need // 2, rows, fourth)
        clear(m2)

        def fifth(a, n):
            parts = [x[:, 0:rows] for x in around(e2, a, n)]
            parts += [m2[a + i : a + i + n, 0:rows] for i in range(3)]
            d1[a + 1 : a + 1 + n, 0:rows] = conv(parts, w5, n, rows)

        ranged(need, pairs - need, rows, fifth)
        clear(d1)

        def sixth(a, n):
            parts = [x[:, 0:rows] for x in around(d1, a, n)]
            d2[a - margin : a - margin + n, 0:rows] = conv(parts, w6, n, rows)

        ranged(margin, pairs - margin, rows, sixth)

        inner = pairs - 2 * margin
        blocks = inner // BLOCK
        line, lane = iota((full, half), 0), iota((full, half), 1)
        aim = (line % half) // 32 * 32 + line // half

        def add(m, head):
            weight = jnp.where(lane == aim + 2 * m, tail[...].astype(F32), 0.0).astype(BF)
            x = jnp.concatenate([d2[b * BLOCK + m, 0:rows] for b in range(blocks)], axis=0)
            return head + dot(x, weight)

        zero = jnp.zeros((blocks * rows, half), F32)
        head = lax.fori_loop(0, BLOCK, add, zero, unroll=small)
        parts_per = BLOCK // per_chunk
        first = margin // per_chunk
        line, lane = iota((128, half), 0), iota((128, half), 1)
        pair, q, z = line // window, (line % window) // levels, line % levels
        picture = jnp.zeros((blocks * rows, half), F32)
        for i in range(parts_per):
            hit = (q > 0) & (q < 3) & (lane == z * 32 + 2 * (i * per_chunk + pair) + q - 1)
            pickout = jnp.where(hit, 1.0, 0.0).astype(BF)
            x = jnp.concatenate([u[first + b * parts_per + i] for b in range(blocks)], axis=0)
            picture = picture + dot(x, pickout)
        return head, picture, blocks

    def windows(source, deep, rows, pairs, offset):
        strip = min(pairs * window, 1024)
        lane, col = iota((deep, strip), 0), iota((deep, strip), 1)
        ahead = lane - offset - 2 * (col // window) - (col % window) // levels
        chunks = []
        for start in range(0, pairs * window, strip):

            def add(z, total, start=start):
                hit = (ahead == 2 * (start // window)) & (col % levels == z)
                return total + dot(source(z), jnp.where(hit, 1.0, 0.0).astype(BF))

            zero = jnp.zeros((rows, strip), F32)
            total = lax.fori_loop(0, levels, add, zero, unroll=small)
            total = total.astype(BF)
            chunks += [total[:, i : i + 128] for i in range(0, strip, 128)]
        return chunks

    own_x.wait()
    loop(slabs, s, lambda k: xin_from(k).wait_recv())
    pairs_x = width // 2 + 2 * HALO
    groups = -(-pairs_x // GROUP)
    lead = 128 + g * width - 2 * HALO - 1
    base_lane = lead // 128 * 128

    def x_source(z):
        return jnp.concatenate(
            [
                vxz[z, :, pl.ds(pl.multiple_of(base_lane + 128 * n, 128), 256)]
                for n in range(groups)
            ],
            axis=0,
        )

    chunk_list = windows(x_source, 256, groups * yd, GROUP, lead - base_lane)
    u = [x[n * yd : (n + 1) * yd] for n in range(groups) for x in chunk_list]
    u = jnp.stack(u[: pairs_x // per_chunk])

    def clear(ref, by=1):
        h, n = HALO // by, pairs_x // by
        zero = jnp.zeros((h, yd, ref.shape[-1]), BF)

        @pl.when(g == 0)
        def _():
            ref[1 : 1 + h, 0:yd] = zero

        @pl.when(g == slabs * chs - 1)
        def _():
            ref[1 + n - h : 1 + n, 0:yd] = zero

    head, picture, blocks = network(u, yd, pairs_x, HALO, clear)
    flag = jnp.concatenate([xz_flag[...]] * blocks, axis=0)
    done = jnp.where(flag[:, 0:1] > 0, picture + head, picture).astype(BF)
    done = done.reshape(blocks, yd, half)
    span = xr.shape[-1]
    per = min(4, blocks)
    skew = lax.rem(g * width, 128)
    line, lane = iota((half, levels * 128), 0), iota((half, levels * 128), 1)
    for n in range(span // 128):
        total = jnp.zeros((yd, levels * 128), F32)
        for b in range(per):
            hit = lane == line // 32 * 128 + skew + 32 * b + line % 32
            total = total + dot(done[n * per + b], jnp.where(hit, 1.0, 0.0).astype(BF))
        total = total.astype(BF)
        for z in range(levels):
            xr[z, :, 128 * n : 128 * (n + 1)] = total[:, 128 * z : 128 * (z + 1)]

    def xo(k):
        return pltpu.make_async_remote_copy(
            src_ref=xr.at[pl.ds(k // chs * zd, zd)],
            dst_ref=rx.at[g],
            send_sem=xo_send.at[k],
            recv_sem=xo_recv.at[g],
            device_id={"slab": k // chs, "tile": t, "ch": k % chs},
            device_id_type=MESH,
        )

    def xo_from(k):
        return pltpu.make_async_remote_copy(
            src_ref=xr.at[pl.ds(k // chs * zd, zd)],
            dst_ref=rx.at[k],
            send_sem=xo_send.at[k],
            recv_sem=xo_recv.at[k],
            device_id={"slab": k // chs, "tile": t, "ch": k % chs},
            device_id_type=MESH,
        )

    loop(slabs * chs, g, lambda k: xo(k).start())
    own_xo = pltpu.make_async_copy(xr.at[pl.ds(s * zd, zd)], rx.at[g], in_local.at[2])
    own_xo.start()

    own_y.wait()
    loop(slabs * tiles, place_me, lambda k: yin_from(k).wait_recv())
    for z in range(levels):
        plane = ryz[:, z // zd, z % zd].reshape(breadth, 128).astype(F32)
        turned[z] = plane.T
    in_block = lax.rem(me * cols, 128)
    row_start = pl.multiple_of(in_block // rows_y * rows_y, rows_y)

    def y_source(z):
        return turned[z, pl.ds(row_start, rows_y), :].astype(BF)

    pairs_y = breadth // 2
    u = jnp.stack(windows(y_source, breadth, rows_y, pairs_y, -1))
    head, picture, blocks = network(u, rows_y, pairs_y, 0, lambda ref, by=1: None)
    row = iota((rows_y, 1), 0) + row_start
    mine = (row >= in_block) & (row < in_block + cols)
    flag = yz_flag[pl.ds(row_start, rows_y), 0:1]
    for b in range(blocks):
        a = slice(b * rows_y, (b + 1) * rows_y)
        got = jnp.where(flag > 0, picture[a] + head[a], picture[a])
        place[...] = jnp.zeros(place.shape, F32)
        place[pl.ds(row_start, rows_y), :] = jnp.where(mine, got, 0.0)
        yt[b] = place[...].T.astype(BF).reshape(levels, 32 // yd, yd, 128)

    fold = 32 // yd

    def yo(k):
        ks, kt, kc = coords(k)
        return pltpu.make_async_remote_copy(
            src_ref=yt.at[kt // fold, pl.ds(ks * zd, zd), lax.rem(kt, fold)],
            dst_ref=ry.at[me],
            send_sem=yo_send.at[k],
            recv_sem=yo_recv.at[me],
            device_id={"slab": ks, "tile": kt, "ch": kc},
            device_id_type=MESH,
        )

    def yo_from(k):
        ks, kt, kc = coords(k)
        return pltpu.make_async_remote_copy(
            src_ref=yt.at[kt // fold, pl.ds(ks * zd, zd), lax.rem(kt, fold)],
            dst_ref=ry.at[k],
            send_sem=yo_send.at[k],
            recv_sem=yo_recv.at[k],
            device_id={"slab": ks, "tile": kt, "ch": kc},
            device_id_type=MESH,
        )

    others(lambda k: yo(k).start())
    own_yo = pltpu.make_async_copy(
        yt.at[t // fold, pl.ds(s * zd, zd), lax.rem(t, fold)], ry.at[me], in_local.at[3]
    )
    own_yo.start()
    own_xo.wait()
    loop(slabs * chs, g, lambda k: xo_from(k).wait_recv())
    own_yo.wait()
    others(lambda k: yo_from(k).wait_recv())
    for b in range(across // 128):
        if width >= 128:
            at = b * 128 % width
            xz = rx[b * 128 // width, :, :, at : at + 128].astype(F32)
        else:
            each = 128 // width
            xz = sum(rx[b * each + i].astype(F32) for i in range(each))
        each = 128 // cols
        yz = sum(ry[b * each + i].astype(F32) for i in range(each))
        out[:, :, 128 * b : 128 * (b + 1)] = (0.5 * (xz + yz)).astype(BF)
    loop(slabs, s, lambda k: xin(k).wait_send())
    loop(slabs * tiles, place_me, lambda k: yin(k).wait_send())
    loop(slabs * chs, g, lambda k: xo(k).wait_send())
    others(lambda k: yo(k).wait_send())


def taps_first(weight):
    return jnp.transpose(weight, (1, 2, 0)).reshape(-1, weight.shape[0])


def per_device(
    volume, xz_tissue, yz_tissue,
    first_conv, second_conv, third_conv, fourth_conv, fifth_conv, sixth_conv, out_weight,
):
    slabs, tiles, chs = (lax.axis_size(name) for name in ("slab", "tile", "ch"))
    zd, yd, across = volume.shape
    levels, breadth = slabs * zd, tiles * yd
    devices = slabs * tiles * chs
    half, full = 32 * levels, 64 * levels
    width, cols = across // (slabs * chs), across // devices
    rows_y = max(16, cols)
    rows = max(yd, rows_y)
    most = max(width // 2 + 2 * HALO, breadth // 2)
    span = max(128, width)
    held = cols * chs
    place = lax.axis_index("slab") * tiles + lax.axis_index("tile")
    xz_flag = jnp.broadcast_to(xz_tissue[:, None], (yd, 128))
    spot = lax.rem(place * held, 128)
    yz_flag = lax.dynamic_update_slice(
        jnp.zeros((128,), jnp.int32), yz_tissue, (spot,)
    )
    yz_flag = jnp.broadcast_to(yz_flag[:, None], (128, 128))
    tail = jnp.broadcast_to(jnp.tile(out_weight, 2 * levels)[:, None], (full, half))
    first = jnp.pad(taps_first(first_conv), ((0, 7), (0, 0)))
    dma = pltpu.SemaphoreType.DMA
    vmem = pl.BlockSpec(memory_space=pltpu.VMEM)

    def act(n, lanes, m=rows):
        return pltpu.VMEM((n, m, lanes), BF)

    return pl.pallas_call(
        functools.partial(kernel, slabs, tiles, chs),
        out_shape=jax.ShapeDtypeStruct((zd, yd, across), BF),
        in_specs=[vmem] * 10,
        out_specs=vmem,
        scratch_shapes=[
            pltpu.VMEM((levels, yd, across + 256), BF),
            pltpu.VMEM((tiles, slabs, zd, yd, 128), BF),
            pltpu.VMEM((levels, 128, breadth), F32),
            pltpu.VMEM((128, 128 // (4 * levels) * full), BF),
            pltpu.VMEM((4 * half, full), BF),
            pltpu.VMEM((4 * half, full), BF),
            pltpu.VMEM((4 * half, full), BF),
            pltpu.VMEM((7 * half, full), BF),
            pltpu.VMEM((4 * half, full), BF),
            act(most + 2, full),
            act(most + 2, full),
            act(most // 2 + 2, full),
            act(most // 2 + 2, full),
            act(most + 2, half),
            pltpu.VMEM((9 * 96, full), F32),
            pltpu.VMEM((levels, yd, span), BF),
            pltpu.VMEM((breadth // 32, levels, 32 // yd, yd, 128), BF),
            pltpu.VMEM((128, half), F32),
            pltpu.VMEM((slabs * chs, zd, yd, span), BF),
            pltpu.VMEM((devices, zd, yd, 128), BF),
            dma((4,)),
            dma((slabs,)), dma((slabs,)),
            dma((slabs * tiles,)), dma((slabs * tiles,)),
            dma((slabs * chs,)), dma((slabs * chs,)),
            dma((devices,)), dma((devices,)),
        ],
        compiler_params=pltpu.CompilerParams(
            collective_id=0, has_side_effects=True, vmem_limit_bytes=58 * 1024 * 1024
        ),
    )(
        volume, xz_flag, yz_flag, first,
        taps_first(second_conv), taps_first(third_conv), taps_first(fourth_conv),
        taps_first(fifth_conv), taps_first(sixth_conv), tail,
    )


def solution(mesh):
    return jax.shard_map(
        per_device,
        mesh=mesh,
        in_specs=(P("slab", "tile", None), P("tile"), P(("slab", "tile"))) + (P(),) * 7,
        out_specs=P("slab", "tile", None),
        check_vma=False,
    )
```

```python
import functools

import jax
import jax.numpy as jnp
from jax import lax
from jax.experimental import pallas as pl
from jax.experimental.pallas import tpu as pltpu
from jax.sharding import PartitionSpec as P

MESH = pl.DeviceIdType.MESH
HALO = 8
GROUP = 64
BLOCK = 16
BF = jnp.bfloat16
F32 = jnp.float32


def iota(shape, axis):
    return lax.broadcasted_iota(jnp.int32, shape, axis)


def dot(a, b):
    return jnp.dot(a, b, preferred_element_type=F32)


def spread(wide, taps):
    count, outs = taps.shape
    lanes = wide.shape[1]
    repeat = jnp.where(iota((outs, lanes), 1) % outs == iota((outs, lanes), 0), 1.0, 0.0)
    wide[0:count, :] = dot(taps, repeat.astype(BF))


def band(dst, row, wide, depth, first, count, spots, pick, disjoint=True):
    p, zo = spots
    total = jnp.zeros((count, wide.shape[1]), F32)
    for r in range(3):
        for s in range(3):
            hit = pick(p, zo, r, s)
            if hit is None:
                continue
            start = (3 * r + s) * depth + first
            tap = wide[start : start + count, :]
            total = jnp.where(hit, tap if disjoint else total + tap, total)
    dst[row : row + count, :] = total.astype(BF)


def plain_pick(q, zi):
    def pick(p, zo, r, s):
        if s not in (q, q - 1):
            return None
        return (p == q - s) & (zo == zi + 1 - r)

    return pick


def up_pick(d, zp):
    def pick(p, zo, r, s):
        return ((p + s + 1) >> 1 == d + 1) & ((zo + r - 1) >> 1 == zp)

    return pick


def kernel(
    slabs, tiles, chs,
    vol, xz_flag, yz_flag, k1, k2, k3, k4, k5, k6, tail,
    out,
    vxz, ryz, turned, w1, w2, w3, w4, w5, w6,
    e1, e2, pooled, m1, m2, wide,
    xr, yt, place, rx, ry,
    in_local, xin_send, xin_recv, yin_send, yin_recv,
    xo_send, xo_recv, yo_send, yo_recv,
):
    d1, d2 = e1, e2
    zd, yd, across = vol.shape
    levels = slabs * zd
    breadth = tiles * yd
    devices = slabs * tiles * chs
    half = 32 * levels
    full = 2 * half
    small = half <= 128
    window = 4 * levels
    per_chunk = 128 // window
    width = across // (slabs * chs)
    cols = across // devices
    rows_y = max(16, cols)
    s, t, c = lax.axis_index("slab"), lax.axis_index("tile"), lax.axis_index("ch")
    g = s * chs + c
    me = (s * tiles + t) * chs + c

    def coords(k):
        return lax.div(k, tiles * chs), lax.rem(lax.div(k, chs), tiles), lax.rem(k, chs)

    def loop(count, own, body):
        def step(i, carry):
            body(lax.rem(own + i, count))
            return carry

        lax.fori_loop(1, count, step, 0)

    def others(body):
        loop(devices, me, body)

    barrier = pltpu.get_barrier_semaphore()

    def greet(k):
        ks, kt, kc = coords(k)
        pl.semaphore_signal(
            barrier, inc=1, device_id={"slab": ks, "tile": kt, "ch": kc}, device_id_type=MESH
        )

    others(greet)
    pl.semaphore_wait(barrier, devices - 1)

    def xin(k):
        return pltpu.make_async_remote_copy(
            src_ref=vol,
            dst_ref=vxz.at[pl.ds(s * zd, zd), :, pl.ds(128, across)],
            send_sem=xin_send.at[k],
            recv_sem=xin_recv.at[s],
            device_id={"slab": k, "tile": t, "ch": c},
            device_id_type=MESH,
        )

    def xin_from(k):
        return pltpu.make_async_remote_copy(
            src_ref=vol,
            dst_ref=vxz.at[pl.ds(k * zd, zd), :, pl.ds(128, across)],
            send_sem=xin_send.at[k],
            recv_sem=xin_recv.at[k],
            device_id={"slab": k, "tile": t, "ch": c},
            device_id_type=MESH,
        )

    def lanes_of(k):
        return pl.ds(pl.multiple_of(lax.div(k * cols * chs, 128) * 128, 128), 128)

    def yin(k):
        ks, kt = lax.div(k, tiles), lax.rem(k, tiles)
        return pltpu.make_async_remote_copy(
            src_ref=vol.at[:, :, lanes_of(k)],
            dst_ref=ryz.at[t, s],
            send_sem=yin_send.at[k],
            recv_sem=yin_recv.at[s * tiles + t],
            device_id={"slab": ks, "tile": kt, "ch": c},
            device_id_type=MESH,
        )

    def yin_from(k):
        ks, kt = lax.div(k, tiles), lax.rem(k, tiles)
        return pltpu.make_async_remote_copy(
            src_ref=vol.at[:, :, lanes_of(k)],
            dst_ref=ryz.at[kt, ks],
            send_sem=yin_send.at[k],
            recv_sem=yin_recv.at[k],
            device_id={"slab": ks, "tile": kt, "ch": c},
            device_id_type=MESH,
        )

    place_me = s * tiles + t
    loop(slabs, s, lambda k: xin(k).start())
    loop(slabs * tiles, place_me, lambda k: yin(k).start())
    own_x = pltpu.make_async_copy(
        vol, vxz.at[pl.ds(s * zd, zd), :, pl.ds(128, across)], in_local.at[0]
    )
    own_y = pltpu.make_async_copy(vol.at[:, :, lanes_of(place_me)], ryz.at[t, s], in_local.at[1])
    own_x.start()
    own_y.start()

    edge = jnp.zeros((levels, yd, 128), BF)
    vxz[:, :, 0:128] = edge
    vxz[:, :, 128 + across :] = edge

    spread(wide, k1[...])
    lane, line = iota((1, full), 1), iota((window, 1), 0)
    side = lane // half
    fine = (side, (lane % half) // 32)
    coarse = (side, (lane % half) // 64)
    step, level = line // levels, line % levels
    base = jnp.zeros((window, full), F32)
    for r in range(3):
        for q in range(3):
            hit = (step - side == q) & (level - fine[1] + 1 == r)
            base = jnp.where(hit, wide[3 * r + q : 3 * r + q + 1, :], base)
    base = base.astype(BF)
    w1[...] = jnp.zeros(w1.shape, BF)
    for m in range(per_chunk):
        w1[m * window : (m + 1) * window, m * full : (m + 1) * full] = base

    order = (1, 2, 0, 3)
    for kk, ww in ((k2, w2), (k6, w6)):
        spread(wide, kk[...])
        for n, q in enumerate(order):
            for zi in range(levels):
                band(ww, n * half + 32 * zi, wide, 32, 0, 32, fine, plain_pick(q, zi))
    spread(wide, k3[...])
    for n, q in enumerate(order):
        for zi in range(levels // 2):
            band(w3, n * half + 64 * zi, wide, 32, 0, 32, coarse, plain_pick(q, zi))
            w3[n * half + 64 * zi + 32 : n * half + 64 * zi + 64, :] = jnp.zeros((32, full), BF)
    spread(wide, k4[...])
    for n, q in enumerate(order):
        for zi in range(levels // 2):
            band(w4, n * half + 64 * zi, wide, 64, 0, 64, coarse, plain_pick(q, zi))
    spread(wide, k5[...])
    for n, q in enumerate(order):
        for zi in range(levels):
            band(w5, n * half + 32 * zi, wide, 96, 64, 32, fine, plain_pick(q, zi))
    for n, d in enumerate((-1, 0, 1)):
        for zp in range(levels // 2):
            band(
                w5, (4 + n) * half + 64 * zp, wide, 96, 0, 64, fine,
                up_pick(d, zp), False,
            )

    def pieces(count, rows):
        best = 1
        for n in range(1, count + 1):
            if count % n == 0 and count // n * rows * half >= 384 * 128:
                best = n
        return best

    def ranged(lo, hi, rows, body):
        n = pieces(hi - lo, rows)
        size = (hi - lo) // n
        for i in range(n):
            body(lo + i * size, size)

    def around(src, a, n):
        return [
            src[a + 1 : a + 1 + n],
            src[a : a + n][:, :, half:],
            src[a + 2 : a + 2 + n][:, :, :half],
        ]

    def conv(parts, weight, n, rows):
        joined = jnp.concatenate(parts, axis=-1)
        joined = joined.reshape(n * rows, joined.shape[-1])
        return jnp.maximum(dot(joined, weight[...]), 0.0).astype(BF).reshape(n, rows, full)

    def network(u, rows, pairs, margin, clear):
        chunks = pairs // per_chunk
        for ref in (e1, e2):
            z1 = jnp.zeros((1, rows, full), BF)
            ref[0:1, 0:rows] = z1
            ref[pairs + 1 : pairs + 2, 0:rows] = z1
        for ref in (pooled, m1):
            z1 = jnp.zeros((1, rows, full), BF)
            ref[0:1, 0:rows] = z1
            ref[pairs // 2 + 1 : pairs // 2 + 2, 0:rows] = z1
        z1 = jnp.zeros((1, rows, half), BF)
        m2[0:1, 0:rows] = z1
        m2[pairs + 1 : pairs + 2, 0:rows] = z1
        flat = u.reshape(chunks * rows, 128)
        for m in range(per_chunk):
            got = jnp.maximum(dot(flat, w1[:, m * full : (m + 1) * full]), 0.0).astype(BF)
            got = got.reshape(chunks, rows, full)
            for i in range(chunks):
                e1[i * per_chunk + m + 1, 0:rows] = got[i]
        clear(e1)
        need = margin // 2

        def second(a, n):
            parts = [x[:, 0:rows] for x in around(e1, a, n)]
            got = conv(parts, w2, n, rows)
            e2[a + 1 : a + 1 + n, 0:rows] = got

        ranged(need, pairs - need, rows, second)
        clear(e2)

        def shrink(a, n):
            x = e2[2 * a + 1 : 2 * a + 1 + 2 * n, 0:rows].astype(F32)
            x = (x[:, :, :half] + x[:, :, half:]).reshape(2 * n * rows, half)
            x = (x + pltpu.roll(x, half - 32, axis=1)) * 0.25
            x = x.astype(BF).reshape(n, 2, rows, half)
            pooled[a + 1 : a + 1 + n, 0:rows] = jnp.concatenate([x[:, 0], x[:, 1]], axis=-1)

        ranged(need // 2, pairs // 2 - need // 2, rows, shrink)

        def third(a, n):
            parts = [x[:, 0:rows] for x in around(pooled, a, n)]
            m1[a + 1 : a + 1 + n, 0:rows] = conv(parts, w3, n, rows)

        ranged(need // 2, pairs // 2 - need // 2, rows, third)
        clear(m1, 2)

        def fourth(a, n):
            parts = [x[:, 0:rows] for x in around(m1, a, n)]
            got = conv(parts, w4, n, rows)
            for i in range(n):
                m2[2 * (a + i) + 1, 0:rows] = got[i, :, :half]
                m2[2 * (a + i) + 2, 0:rows] = got[i, :, half:]

        ranged(need // 2, pairs // 2 - need // 2, rows, fourth)
        clear(m2)

        def fifth(a, n):
            parts = [x[:, 0:rows] for x in around(e2, a, n)]
            parts += [m2[a + i : a + i + n, 0:rows] for i in range(3)]
            d1[a + 1 : a + 1 + n, 0:rows] = conv(parts, w5, n, rows)

        ranged(need, pairs - need, rows, fifth)
        clear(d1)

        def sixth(a, n):
            parts = [x[:, 0:rows] for x in around(d1, a, n)]
            d2[a - margin : a - margin + n, 0:rows] = conv(parts, w6, n, rows)

        ranged(margin, pairs - margin, rows, sixth)

        inner = pairs - 2 * margin
        blocks = inner // BLOCK
        line = iota((full, 1), 0)
        ahead = iota((full, half), 1) - ((line % half) // 32 * 32 + line // half)
        same = line % 32 == iota((1, 32), 1)
        column = jnp.sum(jnp.where(same, tail[...].astype(F32), 0.0), axis=1, keepdims=True)
        column = jnp.broadcast_to(column, (full, half))

        def add(m, head):
            weight = jnp.where(ahead == 2 * m, column, 0.0).astype(BF)
            x = jnp.concatenate([d2[b * BLOCK + m, 0:rows] for b in range(blocks)], axis=0)
            return head + dot(x, weight)

        zero = jnp.zeros((blocks * rows, half), F32)
        head = lax.fori_loop(0, BLOCK, add, zero, unroll=small)
        parts_per = BLOCK // per_chunk
        first = margin // per_chunk
        line = iota((128, 1), 0)
        pair, q, z = line // window, (line % window) // levels, line % levels
        aim = jnp.where((q > 0) & (q < 3), z * 32 + 2 * pair + q - 1, -4 * half)
        past = iota((128, half), 1) - aim
        picture = jnp.zeros((blocks * rows, half), F32)
        for i in range(parts_per):
            pickout = jnp.where(past == 2 * i * per_chunk, 1.0, 0.0).astype(BF)
            x = jnp.concatenate([u[first + b * parts_per + i] for b in range(blocks)], axis=0)
            picture = picture + dot(x, pickout)
        return head, picture, blocks

    def windows(source, deep, rows, pairs, offset):
        strip = min(pairs * window, 1024)
        lane, col = iota((deep, strip), 0), iota((1, strip), 1)
        reach = offset + 2 * (col // window) + (col % window) // levels
        level = col % levels
        chunks = []
        for start in range(0, pairs * window, strip):

            def add(z, total, start=start):
                spot = jnp.where(level == z, reach + 2 * (start // window), -1)
                return total + dot(source(z), jnp.where(lane == spot, 1.0, 0.0).astype(BF))

            zero = jnp.zeros((rows, strip), F32)
            total = lax.fori_loop(0, levels, add, zero, unroll=small)
            total = total.astype(BF)
            chunks += [total[:, i : i + 128] for i in range(0, strip, 128)]
        return chunks

    own_x.wait()
    loop(slabs, s, lambda k: xin_from(k).wait_recv())
    pairs_x = width // 2 + 2 * HALO
    groups = -(-pairs_x // GROUP)
    lead = 128 + g * width - 2 * HALO - 1
    base_lane = lead // 128 * 128

    def x_source(z):
        return jnp.concatenate(
            [
                vxz[z, :, pl.ds(pl.multiple_of(base_lane + 128 * n, 128), 256)]
                for n in range(groups)
            ],
            axis=0,
        )

    chunk_list = windows(x_source, 256, groups * yd, GROUP, lead - base_lane)
    u = [x[n * yd : (n + 1) * yd] for n in range(groups) for x in chunk_list]
    u = jnp.stack(u[: pairs_x // per_chunk])

    def clear(ref, by=1):
        h, n = HALO // by, pairs_x // by
        zero = jnp.zeros((h, yd, ref.shape[-1]), BF)

        @pl.when(g == 0)
        def _():
            ref[1 : 1 + h, 0:yd] = zero

        @pl.when(g == slabs * chs - 1)
        def _():
            ref[1 + n - h : 1 + n, 0:yd] = zero

    head, picture, blocks = network(u, yd, pairs_x, HALO, clear)
    same = iota((yd, yd), 0) == iota((yd, yd), 1)
    flag = jnp.sum(jnp.where(same, xz_flag[...].astype(F32), 0.0), axis=1, keepdims=True)
    flag = jnp.concatenate([flag] * blocks, axis=0)
    done = jnp.where(flag > 0, picture + head, picture).astype(BF)
    done = done.reshape(blocks, yd, half)
    span = xr.shape[-1]
    per = min(4, blocks)
    skew = lax.rem(g * width, 128)
    line = iota((half, 1), 0)
    past = iota((half, levels * 128), 1) - (line // 32 * 128 + skew + line % 32)
    for n in range(span // 128):
        total = jnp.zeros((yd, levels * 128), F32)
        for b in range(per):
            hit = jnp.where(past == 32 * b, 1.0, 0.0).astype(BF)
            total = total + dot(done[n * per + b], hit)
        total = total.astype(BF)
        for z in range(levels):
            xr[z, :, 128 * n : 128 * (n + 1)] = total[:, 128 * z : 128 * (z + 1)]

    def xo(k):
        return pltpu.make_async_remote_copy(
            src_ref=xr.at[pl.ds(lax.div(k, chs) * zd, zd)],
            dst_ref=rx.at[g],
            send_sem=xo_send.at[k],
            recv_sem=xo_recv.at[g],
            device_id={"slab": lax.div(k, chs), "tile": t, "ch": lax.rem(k, chs)},
            device_id_type=MESH,
        )

    def xo_from(k):
        return pltpu.make_async_remote_copy(
            src_ref=xr.at[pl.ds(lax.div(k, chs) * zd, zd)],
            dst_ref=rx.at[k],
            send_sem=xo_send.at[k],
            recv_sem=xo_recv.at[k],
            device_id={"slab": lax.div(k, chs), "tile": t, "ch": lax.rem(k, chs)},
            device_id_type=MESH,
        )

    loop(slabs * chs, g, lambda k: xo(k).start())
    own_xo = pltpu.make_async_copy(xr.at[pl.ds(s * zd, zd)], rx.at[g], in_local.at[2])
    own_xo.start()

    own_y.wait()
    loop(slabs * tiles, place_me, lambda k: yin_from(k).wait_recv())
    for z in range(levels):
        plane = ryz[:, z // zd, z % zd].reshape(breadth, 128).astype(F32)
        turned[z] = plane.T
    in_block = lax.rem(me * cols, 128)
    row_start = pl.multiple_of(in_block // rows_y * rows_y, rows_y)

    def y_source(z):
        return turned[z, pl.ds(row_start, rows_y), :].astype(BF)

    pairs_y = breadth // 2
    u = jnp.stack(windows(y_source, breadth, rows_y, pairs_y, -1))
    head, picture, blocks = network(u, rows_y, pairs_y, 0, lambda ref, by=1: None)
    row = iota((rows_y, 1), 0) + row_start
    mine = (row >= in_block) & (row < in_block + cols)
    held = yz_flag.shape[1]
    shift = row_start - lax.rem(place_me * held, 128)
    same = iota((rows_y, held), 0) + shift == iota((rows_y, held), 1)
    flag = jnp.sum(jnp.where(same, yz_flag[...].astype(F32), 0.0), axis=1, keepdims=True)
    for b in range(blocks):
        a = slice(b * rows_y, (b + 1) * rows_y)
        got = jnp.where(flag > 0, picture[a] + head[a], picture[a])
        place[...] = jnp.zeros(place.shape, F32)
        place[pl.ds(row_start, rows_y), :] = jnp.where(mine, got, 0.0)
        yt[b] = place[...].T.astype(BF).reshape(levels, 32 // yd, yd, 128)

    fold = 32 // yd

    def yo(k):
        ks, kt, kc = coords(k)
        return pltpu.make_async_remote_copy(
            src_ref=yt.at[lax.div(kt, fold), pl.ds(ks * zd, zd), lax.rem(kt, fold)],
            dst_ref=ry.at[me],
            send_sem=yo_send.at[k],
            recv_sem=yo_recv.at[me],
            device_id={"slab": ks, "tile": kt, "ch": kc},
            device_id_type=MESH,
        )

    def yo_from(k):
        ks, kt, kc = coords(k)
        return pltpu.make_async_remote_copy(
            src_ref=yt.at[lax.div(kt, fold), pl.ds(ks * zd, zd), lax.rem(kt, fold)],
            dst_ref=ry.at[k],
            send_sem=yo_send.at[k],
            recv_sem=yo_recv.at[k],
            device_id={"slab": ks, "tile": kt, "ch": kc},
            device_id_type=MESH,
        )

    others(lambda k: yo(k).start())
    own_yo = pltpu.make_async_copy(
        yt.at[t // fold, pl.ds(s * zd, zd), lax.rem(t, fold)], ry.at[me], in_local.at[3]
    )
    own_yo.start()
    own_xo.wait()
    loop(slabs * chs, g, lambda k: xo_from(k).wait_recv())
    own_yo.wait()
    others(lambda k: yo_from(k).wait_recv())
    for b in range(across // 128):
        if width >= 128:
            at = b * 128 % width
            xz = rx[b * 128 // width, :, :, at : at + 128].astype(F32)
        else:
            each = 128 // width
            xz = sum(rx[b * each + i].astype(F32) for i in range(each))
        each = 128 // cols
        yz = sum(ry[b * each + i].astype(F32) for i in range(each))
        out[:, :, 128 * b : 128 * (b + 1)] = (0.5 * (xz + yz)).astype(BF)
    loop(slabs, s, lambda k: xin(k).wait_send())
    loop(slabs * tiles, place_me, lambda k: yin(k).wait_send())
    loop(slabs * chs, g, lambda k: xo(k).wait_send())
    others(lambda k: yo(k).wait_send())


def taps_first(weight):
    return jnp.transpose(weight, (1, 2, 0)).reshape(-1, weight.shape[0])


def per_device(
    volume, xz_tissue, yz_tissue,
    first_conv, second_conv, third_conv, fourth_conv, fifth_conv, sixth_conv, out_weight,
):
    slabs, tiles, chs = (lax.axis_size(name) for name in ("slab", "tile", "ch"))
    zd, yd, across = volume.shape
    levels, breadth = slabs * zd, tiles * yd
    devices = slabs * tiles * chs
    half, full = 32 * levels, 64 * levels
    width, cols = across // (slabs * chs), across // devices
    rows_y = max(16, cols)
    rows = max(yd, rows_y)
    most = max(width // 2 + 2 * HALO, breadth // 2)
    span = max(128, width)
    xz_flag = xz_tissue.reshape(1, -1)
    yz_flag = yz_tissue.reshape(1, -1)
    tail = out_weight.reshape(1, -1)
    first = jnp.pad(taps_first(first_conv), ((0, 7), (0, 0)))
    dma = pltpu.SemaphoreType.DMA
    vmem = pl.BlockSpec(memory_space=pltpu.VMEM)

    def act(n, lanes, m=rows):
        return pltpu.VMEM((n, m, lanes), BF)

    return pl.pallas_call(
        functools.partial(kernel, slabs, tiles, chs),
        out_shape=jax.ShapeDtypeStruct((zd, yd, across), BF),
        in_specs=[vmem] * 10,
        out_specs=vmem,
        scratch_shapes=[
            pltpu.VMEM((levels, yd, across + 256), BF),
            pltpu.VMEM((tiles, slabs, zd, yd, 128), BF),
            pltpu.VMEM((levels, 128, breadth), F32),
            pltpu.VMEM((128, 128 // (4 * levels) * full), BF),
            pltpu.VMEM((4 * half, full), BF),
            pltpu.VMEM((4 * half, full), BF),
            pltpu.VMEM((4 * half, full), BF),
            pltpu.VMEM((7 * half, full), BF),
            pltpu.VMEM((4 * half, full), BF),
            act(most + 2, full),
            act(most + 2, full),
            act(most // 2 + 2, full),
            act(most // 2 + 2, full),
            act(most + 2, half),
            pltpu.VMEM((9 * 96, full), F32),
            pltpu.VMEM((levels, yd, span), BF),
            pltpu.VMEM((breadth // 32, levels, 32 // yd, yd, 128), BF),
            pltpu.VMEM((128, half), F32),
            pltpu.VMEM((slabs * chs, zd, yd, span), BF),
            pltpu.VMEM((devices, zd, yd, 128), BF),
            dma((4,)),
            dma((slabs,)), dma((slabs,)),
            dma((slabs * tiles,)), dma((slabs * tiles,)),
            dma((slabs * chs,)), dma((slabs * chs,)),
            dma((devices,)), dma((devices,)),
        ],
        compiler_params=pltpu.CompilerParams(
            collective_id=0, has_side_effects=True, vmem_limit_bytes=58 * 1024 * 1024
        ),
    )(
        volume, xz_flag, yz_flag, first,
        taps_first(second_conv), taps_first(third_conv), taps_first(fourth_conv),
        taps_first(fifth_conv), taps_first(sixth_conv), tail,
    )


def solution(mesh):
    return jax.shard_map(
        per_device,
        mesh=mesh,
        in_specs=(P("slab", "tile", None), P("tile"), P(("slab", "tile"))) + (P(),) * 7,
        out_specs=P("slab", "tile", None),
        check_vma=False,
    )
```
